32 devices in a mesh: kpt: 2 (over y), row: 4 (over z), col: 2 (over x), sub: 2 (over core).
Axes of the slice: x: 2, y: 2, z: 4, core: 2. Of those that a mesh axis runs over, the one named last changes fastest.
Arguments:
- vectors: bfloat16 [3072, 8192], P(('kpt', 'col', 'sub'), 'row'), parts along dimension 0, may hold values from -6 to 6
- blocks: bfloat16 [128, 8, 128, 128], P(('kpt', 'row')), parts along dimension 0, may hold values from -0.0625 to 0.0625
- onsite: float32 [16384], P(('kpt', 'row')), parts along dimension 0, may hold values from -1 to 1
- block_cols: int32 [128, 8], P(('kpt', 'row')), parts along dimension 0, may hold values from 0 to 63, as said below
Outputs:
- correlation: float32 [3072, 1536], P(('kpt', 'row'), ('col', 'sub')), parts along dimension 0
- projected: float32 [3072, 1536], P(('kpt', 'row'), ('col', 'sub')), parts along dimension 0
The draws below stay inside these ranges and needn't reach their ends.
There are 2 independent parts, one for each index of `kpt`. The reference program is written for one: setup_inputs(seed, part) draws one part's arguments, and reference() takes and returns one part's arrays. A program takes and returns all parts, laid end to end along the dimension named above; each array names one. Nothing has to cross between parts.
Inputs may be any that keep to these rules, and one draw needn't show every extreme that they name: `block_cols`: each row holds 8 different block columns: the first is the row's own block, the others lie within 4 blocks of it, counted cyclically over 64 blocks, and every row has one at a distance of exactly 4.
All inputs are finite; a program needn't handle non-finite values.
Results may differ from the reference program's by a relative error of at most 0.01.
Values may be sent and summed in bfloat16 or wider, within the bound.
No kernel may reach another device: no remote copies, remote signals or barrier semaphores. Data moves between devices by JAX's collectives and lax.ppermute only.
A program may use at most 128 MiB of HBM per device.

```python
import jax
import jax.numpy as jnp
from jax import lax

BS = 128
M = 1536
BAND = 4
KB = 8
DEG = 8
NB = 64
N = 8192


def draw_block_cols(key, part):
    key = jax.random.fold_in(key, 7)
    scores = jax.random.randint(key, (NB, 2 * BAND), 0, 1 << 20) * (2 * BAND) + jnp.arange(2 * BAND, dtype=jnp.int32)[None, :]
    ordering = jnp.argsort(scores, axis=1)
    candidates = jnp.concatenate([jnp.arange(-BAND, 0, dtype=jnp.int32), jnp.arange(1, BAND + 1, dtype=jnp.int32)])
    chosen = candidates[ordering[:, :KB - 1]]
    offsets = jnp.concatenate([jnp.zeros((NB, 1), jnp.int32), chosen], axis=1)
    return ((jnp.arange(NB, dtype=jnp.int32)[:, None] + offsets) % NB).astype(jnp.int32)


def block_scale(own_key, dims, cuts, smallest, largest):
    def one(axis_at, parts):
        steps = jax.random.uniform(jax.random.fold_in(jax.random.fold_in(own_key, 6), axis_at), (parts,), jnp.float32, smallest / len(cuts), largest / len(cuts))
        return jnp.repeat(jnp.exp(steps), dims[axis_at] // parts).reshape((-1,) + (1,) * (len(dims) - axis_at - 1))

    loudness = one(*cuts[0])
    for cut in cuts[1:]:
        loudness = loudness * one(*cut)
    return loudness


def gaussian(own_key, dims, spread, bound, split=(), kind=jnp.bfloat16):
    array = spread * jax.random.normal(own_key, dims, jnp.float32)
    if split:
        array = array * block_scale(own_key, dims, split, -0.22, 0.18)
    return jnp.clip(array, -bound, bound).astype(kind)


def setup_inputs(seed: int = 0, part: int = 0) -> dict:
    arg_keys = jax.random.split(jax.random.key(seed), 5)
    own_keys = jax.random.split(jax.random.fold_in(arg_keys[4], part), 5)
    return {
        "vectors": gaussian(own_keys[0], (M, N), 1.0, 6.0, ((0, 4), (1, 4))),
        "blocks": gaussian(own_keys[1], (NB, KB, BS, BS), (10 * KB * BS) ** -0.5, 0.0625, ((0, 4),)),
        "onsite": jnp.clip(jax.random.uniform(own_keys[2], (N,), jnp.float32, -1.0, 1.0) * block_scale(own_keys[2], (N,), ((0, 4),), -0.4, 0.0), -1.0, 1.0),
        "block_cols": draw_block_cols(jax.random.fold_in(jax.random.fold_in(arg_keys[4], part), 71), part),
    }


center = 0.4
half_width = 0.8
lowest = -1.3
gram_weight = 8.0


def apply_hamiltonian(vector_field, blocks, onsite, block_cols):
    shaped = vector_field.reshape(M, NB, BS)

    def block_row(row_block):
        columns = block_cols[row_block]
        picked = shaped[:, columns, :].astype(jnp.float32)
        return jnp.einsum("mkj,kij->mi", picked, blocks[row_block].astype(jnp.float32))

    product = lax.map(block_row, jnp.arange(NB, dtype=jnp.int32))
    product = jnp.transpose(product, (1, 0, 2)).reshape(M, N)
    return product + onsite[None, :] * vector_field.astype(jnp.float32)


def reference(vectors, blocks, onsite, block_cols):
    ratio_first = half_width / (lowest - center)
    twice_inverse = 2.0 / ratio_first
    previous = vectors
    current = ((apply_hamiltonian(previous, blocks, onsite, block_cols) - center * previous.astype(jnp.float32)) * (ratio_first / half_width)).astype(jnp.bfloat16)
    ratio_old = ratio_first
    for degree_step in range(1, DEG):
        ratio_new = 1.0 / (twice_inverse - ratio_old)
        shifted = apply_hamiltonian(current, blocks, onsite, block_cols) - center * current.astype(jnp.float32)
        following = (2.0 * ratio_new / half_width) * shifted - (ratio_old * ratio_new) * previous.astype(jnp.float32)
        previous, current = current, following.astype(jnp.bfloat16)
        ratio_old = ratio_new
    applied = apply_hamiltonian(current, blocks, onsite, block_cols).astype(jnp.bfloat16)
    correlation = jnp.dot(current, current.T, preferred_element_type=jnp.float32) * (gram_weight / N)
    projected = jnp.dot(current, applied.T, preferred_element_type=jnp.float32) * (gram_weight / N)
    return correlation, projected
```

```python
import functools

import jax
import jax.numpy as jnp
from jax import lax
from jax.experimental import pallas as pl
from jax.experimental.pallas import tpu as pltpu
from jax.sharding import PartitionSpec as P

BAND = 4
DEG = 8
PAIR = 2
CHUNKS = 2


center = 0.4
half_width = 0.8
lowest = -1.3
gram_weight = 8.0


def dense_kernel(slots, blocks, out, *, bs, stored):
    pair = pl.program_id(0)
    out[...] = jnp.zeros_like(out)
    for sub_row in range(PAIR):
        for k in range(stored):
            at = pl.multiple_of(slots[(pair * PAIR + sub_row) * stored + k] * bs, bs)
            out[0, pl.ds(at, bs), sub_row * bs:(sub_row + 1) * bs] = blocks[sub_row, k].T


def make_dense(blocks, slots):
    rb, stored, bs, _ = blocks.shape
    pairs = rb // PAIR
    window = (PAIR + 2 * BAND) * bs
    return pl.pallas_call(
        functools.partial(dense_kernel, bs=bs, stored=stored),
        grid_spec=pltpu.PrefetchScalarGridSpec(
            num_scalar_prefetch=1,
            grid=(pairs,),
            in_specs=[pl.BlockSpec((PAIR, stored, bs, bs), lambda p, s: (p, 0, 0, 0))],
            out_specs=pl.BlockSpec((1, window, PAIR * bs), lambda p, s: (p, 0, 0)),
        ),
        out_shape=jax.ShapeDtypeStruct((pairs, window, PAIR * bs), blocks.dtype),
        name="dense_band",
    )(slots, blocks)


def apply_kernel(*refs, halo, shift, alpha, beta, has_prev, has_edges):
    refs = list(refs)
    low, own, high, dense, onsite = refs[:5]
    refs = refs[5:]
    prev = refs.pop(0) if has_prev else None
    out = refs.pop(0)
    step = pl.program_id(0)
    pairs = pl.num_programs(0)
    width = out.shape[1]
    n_loc = own.shape[1]
    window = dense.shape[1]

    def finish(p, product):
        own_here = own[:, p * width:(p + 1) * width].astype(jnp.float32)
        value = product + (onsite[:, p * width:(p + 1) * width] - shift) * own_here
        if alpha != 1.0:
            value = alpha * value
        if has_prev:
            value = value - beta * prev[...].astype(jnp.float32)
        value = value.astype(out.dtype)
        out[...] = value
        if has_edges:
            low_edge, high_edge = refs
            at = p * width
            if at < halo:
                low_edge[:, at:at + width] = value
            if at >= n_loc - halo:
                high_edge[:, at - (n_loc - halo):at - (n_loc - halo) + width] = value

    for p in range(n_loc // width):

        @pl.when(step == p)
        def _(p=p):
            begin = p * width
            total = None
            for ref, first, last in ((low, 0, halo), (own, halo, halo + n_loc), (high, halo + n_loc, 2 * halo + n_loc)):
                lo, hi = max(first, begin), min(last, begin + window)
                if lo < hi:
                    part = jnp.dot(
                        ref[:, lo - first:hi - first],
                        dense[0, lo - begin:hi - begin, :],
                        preferred_element_type=jnp.float32,
                    )
                    total = part if total is None else total + part
            finish(p, total)


def apply_step(low, own, high, dense, onsite, prev, *, shift, alpha, beta, has_edges):
    rows, n_loc = own.shape
    pairs, window, width = dense.shape
    halo = low.shape[1]
    whole = lambda p: (0, 0)
    tile = pl.BlockSpec((rows, width), lambda p: (0, p))
    in_specs = [
        pl.BlockSpec((rows, halo), whole),
        pl.BlockSpec((rows, n_loc), whole),
        pl.BlockSpec((rows, halo), whole),
        pl.BlockSpec((1, window, width), lambda p: (p, 0, 0)),
        pl.BlockSpec((1, n_loc), whole),
    ]
    args = [low, own, high, dense, onsite]
    if prev is not None:
        in_specs.append(tile)
        args.append(prev)
    out_shape = [jax.ShapeDtypeStruct((rows, n_loc), own.dtype)]
    out_specs = [tile]
    if has_edges:
        out_shape += [jax.ShapeDtypeStruct((rows, halo), own.dtype)] * 2
        out_specs += [pl.BlockSpec((rows, halo), whole)] * 2
    return pl.pallas_call(
        functools.partial(
            apply_kernel,
            halo=halo,
            shift=shift,
            alpha=alpha,
            beta=beta,
            has_prev=prev is not None,
            has_edges=has_edges,
        ),
        grid=(pairs,),
        in_specs=in_specs,
        out_specs=out_specs,
        out_shape=out_shape,
        cost_estimate=pl.CostEstimate(
            flops=2 * rows * window * n_loc,
            bytes_accessed=2 * (pairs * window * width + 4 * rows * n_loc),
            transcendentals=0,
        ),
        compiler_params=pltpu.CompilerParams(vmem_limit_bytes=24 * 2**20),
        name="apply_step",
    )(*args)


def gram_kernel(left, *refs, scale, count):
    rights, outs = refs[:count], refs[count:]
    for right, out in zip(rights, outs):
        out[...] = scale * lax.dot_general(
            left[...], right[...], (((1,), (1,)), ((), ())), preferred_element_type=jnp.float32
        )


def gram(left, rights, scale):
    rows, n_loc = left.shape
    cols = rights[0].shape[0]
    count = len(rights)
    return pl.pallas_call(
        functools.partial(gram_kernel, scale=scale, count=count),
        out_shape=[jax.ShapeDtypeStruct((rows, cols), jnp.float32)] * count,
        cost_estimate=pl.CostEstimate(
            flops=2 * rows * cols * n_loc * count,
            bytes_accessed=2 * (rows + cols * count) * n_loc + 4 * rows * cols * count,
            transcendentals=0,
        ),
        compiler_params=pltpu.CompilerParams(vmem_limit_bytes=24 * 2**20),
        name="gram",
    )(left, *rights)


def line_reduce_scatter(terms, axis):
    count = lax.axis_size(axis)
    at = lax.axis_index(axis)

    def pick(target):
        return lax.dynamic_index_in_dim(terms, jnp.clip(target, 0, count - 1), 0, keepdims=False)

    up = down = None
    for step in range(count - 1):
        far = count - 1 - step
        up_target = far + at
        send = pick(up_target)
        if up is not None:
            send = jnp.where(at > 0, up.astype(jnp.float32), 0.0) + send
        up = lax.ppermute(send.astype(jnp.bfloat16), axis, [(z, z + 1) for z in range(step + 1)])
        down_target = at - far
        send = pick(down_target)
        if down is not None:
            send = jnp.where(at < count - 1, down.astype(jnp.float32), 0.0) + send
        down = lax.ppermute(
            send.astype(jnp.bfloat16), axis, [(count - 1 - z, count - 2 - z) for z in range(step + 1)]
        )
    return pick(at) + up.astype(jnp.float32) + down.astype(jnp.float32)


def body(vectors, blocks, onsite, block_cols):
    row_count = lax.axis_size("row")
    position = lax.axis_index("row")
    rb_dev = blocks.shape[0]
    bs_width = blocks.shape[2]
    m_loc, n_loc = vectors.shape
    total_blocks = rb_dev * row_count
    halo = BAND * bs_width
    global_rows = position * rb_dev + jnp.arange(rb_dev, dtype=jnp.int32)
    offset = (
        block_cols - global_rows[:, None] + total_blocks // 2
    ) % total_blocks - total_blocks // 2
    slots = offset + BAND + (jnp.arange(rb_dev, dtype=jnp.int32) % PAIR)[:, None]
    onsite = onsite[None, :]

    forward = [(i, (i + 1) % row_count) for i in range(row_count)]
    backward = [(target, source) for source, target in forward]

    def exchange(low_edge, high_edge):
        return lax.ppermute(high_edge, "row", forward), lax.ppermute(low_edge, "row", backward)

    rows = m_loc // CHUNKS
    current = [vectors[c * rows:(c + 1) * rows] for c in range(CHUNKS)]
    halos = [exchange(x[:, :halo], x[:, n_loc - halo:]) for x in current]
    dense = make_dense(blocks, slots.reshape(-1))

    ratio_first = half_width / (lowest - center)
    twice_inverse = 2.0 / ratio_first
    previous = [None] * CHUNKS
    ratio_old = ratio_first
    alpha, beta = ratio_first / half_width, 0.0
    for degree_step in range(DEG):
        if degree_step:
            ratio_new = 1.0 / (twice_inverse - ratio_old)
            alpha, beta = 2.0 * ratio_new / half_width, ratio_old * ratio_new
            ratio_old = ratio_new
        for c in range(CHUNKS):
            low, high = halos[c]
            following, low_edge, high_edge = apply_step(
                low, current[c], high, dense, onsite, previous[c], shift=center, alpha=alpha, beta=beta, has_edges=True
            )
            previous[c], current[c] = current[c], following
            halos[c] = exchange(low_edge, high_edge)

    cols, subs = lax.axis_size("col"), lax.axis_size("sub")
    col_at, sub_at = lax.axis_index("col"), lax.axis_index("sub")
    peers = {}
    for dc in range(cols):
        moved = current
        if dc:
            turn = [((i + dc) % cols, i) for i in range(cols)]
            moved = [lax.ppermute(x, "col", turn) for x in current]
        for ds in range(subs):
            turn = [((i + ds) % subs, i) for i in range(subs)]
            peers[dc, ds] = [lax.ppermute(x, "sub", turn) for x in moved] if ds else moved

    applied = []
    for c in range(CHUNKS):
        low, high = halos[c]
        (value,) = apply_step(
            low, current[c], high, dense, onsite, None, shift=0.0, alpha=1.0, beta=0.0, has_edges=False
        )
        applied.append(value)

    scale = gram_weight / (n_loc * row_count)

    def terms_of(rights):
        right = jnp.concatenate(rights, axis=0)
        stacked = []
        for dc in range(cols):
            for ds in range(subs):
                stacked.append(jnp.concatenate([gram(left, [right], scale)[0] for left in peers[dc, ds]], axis=0))
        stacked = jnp.stack(stacked)
        absolute = jnp.arange(cols * subs, dtype=jnp.int32)
        relative = ((absolute // subs - col_at) % cols) * subs + (absolute % subs - sub_at) % subs
        return stacked[relative].reshape(row_count, -1, m_loc)

    correlation = line_reduce_scatter(terms_of(current), "row")
    projected = line_reduce_scatter(terms_of(applied), "row")
    return (correlation, projected)


def solution(mesh):
    placed = (
        P(("kpt", "col", "sub"), "row"),
        P(("kpt", "row"), None, None, None),
        P(("kpt", "row")),
        P(("kpt", "row"), None),
    )
    return jax.shard_map(
        body,
        mesh=mesh,
        in_specs=placed,
        out_specs=(P(("kpt", "row"), ("col", "sub")), P(("kpt", "row"), ("col", "sub"))),
        check_vma=False,
    )
```

```python
import functools

import jax
import jax.numpy as jnp
from jax import lax
from jax.experimental import pallas as pl
from jax.experimental.pallas import tpu as pltpu
from jax.sharding import PartitionSpec as P

BAND = 4
DEG = 8
PAIR = 2
CORES = 2
COST = 1


center = 0.4
half_width = 0.8
lowest = -1.3
gram_weight = 8.0


def dense_kernel(info, slots, blocks, out, *, bs, stored):
    pair = pl.program_id(0)
    first = (info[0] * pl.num_programs(0) + pair) * PAIR
    out[...] = jnp.zeros_like(out)
    for sub_row in range(PAIR):
        for k in range(stored):
            at = pl.multiple_of(slots[(first + sub_row) * stored + k] * bs, bs)
            out[0, pl.ds(at, bs), sub_row * bs:(sub_row + 1) * bs] = blocks[sub_row, k].T


def make_dense(info, slots, blocks):
    rb, stored, bs, _ = blocks.shape
    pairs = rb // CORES // PAIR
    window = (PAIR + 2 * BAND) * bs
    return pl.pallas_call(
        functools.partial(dense_kernel, bs=bs, stored=stored),
        grid_spec=pltpu.PrefetchScalarGridSpec(
            num_scalar_prefetch=2,
            grid=(pairs,),
            in_specs=[pl.BlockSpec((PAIR, stored, bs, bs), lambda p, i, s: (i[0] * pairs + p, 0, 0, 0))],
            out_specs=pl.BlockSpec((1, window, PAIR * bs), lambda p, i, s: (p, 0, 0)),
        ),
        out_shape=jax.ShapeDtypeStruct((pairs, window, PAIR * bs), blocks.dtype),
        compiler_params=pltpu.CompilerParams(vmem_limit_bytes=8 * 2**20),
        name="dense_band",
    )(info, slots, blocks)


def apply_kernel(info, *refs, shift, alpha, beta, has_prev, has_whole):
    refs = list(refs)
    line_halo, core_halo, line_part, core_part, dense, onsite = refs[:6]
    refs = refs[6:]
    prev = None
    if has_prev:
        prev, refs = refs[:2], refs[2:]
    out_line, out_core = refs[:2]
    rows, halo = line_part.shape
    pairs, window, width = dense.shape
    core = info[0]

    def run(pieces, prev_pieces, out_pieces):
        for p in range(pairs):
            begin = p * width
            total = None
            for at, ref in enumerate(pieces):
                lo, hi = max(at * halo, begin), min((at + 1) * halo, begin + window)
                if lo < hi:
                    part = jnp.dot(
                        ref[:, lo - at * halo:hi - at * halo],
                        dense[p, lo - begin:hi - begin, :],
                        preferred_element_type=jnp.float32,
                    )
                    total = part if total is None else total + part
            half, inside = divmod(begin, halo)
            here = slice(inside, inside + width)
            diagonal = onsite[:, begin:begin + width] - shift
            value = total + diagonal * pieces[1 + half][:, here].astype(jnp.float32)
            if alpha != 1.0:
                value = alpha * value
            if prev_pieces is not None:
                value = value - beta * prev_pieces[half][:, here].astype(jnp.float32)
            value = value.astype(out_line.dtype)
            out_pieces[half][:, here] = value
            if has_whole:
                refs[2][:, begin:begin + width] = value

    @pl.when(core == 0)
    def _():
        run((line_halo, line_part, core_part, core_halo), prev, (out_line, out_core))

    @pl.when(core != 0)
    def _():
        run((core_halo, core_part, line_part, line_halo), prev and prev[::-1], (out_core, out_line))


def cost(flops, nbytes):
    return pl.CostEstimate(flops=flops // COST, bytes_accessed=nbytes // COST, transcendentals=0)


def local(kernel, info, args, out_shape, flops, name):
    nbytes = sum(x.size * x.dtype.itemsize for x in [*args, *out_shape])
    vmem = pl.BlockSpec(memory_space=pltpu.VMEM)
    return pl.pallas_call(
        kernel,
        in_specs=[pl.BlockSpec(memory_space=pltpu.SMEM)] + [vmem] * len(args),
        out_specs=[vmem] * len(out_shape),
        out_shape=out_shape,
        cost_estimate=cost(flops, nbytes),
        compiler_params=pltpu.CompilerParams(vmem_limit_bytes=20 * 2**20),
        name=name,
    )(info, *args)


def apply_step(info, halos, parts, dense, onsite, prev, *, shift, alpha, beta, has_whole):
    rows, halo = parts[0].shape
    pairs, window, width = dense.shape
    dtype = parts[0].dtype
    out_shape = [jax.ShapeDtypeStruct((rows, halo), dtype)] * 2
    if has_whole:
        out_shape = out_shape + [jax.ShapeDtypeStruct((rows, 2 * halo), dtype)]
    kernel = functools.partial(
        apply_kernel, shift=shift, alpha=alpha, beta=beta, has_prev=prev is not None, has_whole=has_whole
    )
    args = [*halos, *parts, dense, onsite, *(prev or ())]
    return local(kernel, info, args, out_shape, 2 * rows * window * width * pairs, "apply_step")


def gram_kernel(info, *refs, scale):
    lefts, rights, keep, send = refs[:-4], refs[-4:-2], refs[-2], refs[-1]

    def run(mine, other):
        row = 0
        for left in lefts:
            rows = left.shape[0]
            for right, out in ((other, send), (mine, keep)):
                term = lax.dot_general(
                    left[...], right[...], (((1,), (1,)), ((), ())), preferred_element_type=jnp.float32
                )
                out[row:row + rows, :] = (scale * term).astype(out.dtype)
            row += rows

    @pl.when(info[0] == 0)
    def _():
        run(rights[0], rights[1])

    @pl.when(info[0] != 0)
    def _():
        run(rights[1], rights[0])


def gram_terms(info, lefts, rights, scale):
    rows = sum(x.shape[0] for x in lefts)
    cols, width = rights[0].shape
    out_shape = [jax.ShapeDtypeStruct((rows, cols), jnp.float32), jax.ShapeDtypeStruct((rows, cols), jnp.bfloat16)]
    kernel = functools.partial(gram_kernel, scale=scale)
    return local(kernel, info, [*lefts, *rights], out_shape, 4 * rows * cols * width, "gram_terms")


def body(vectors, blocks, onsite, block_cols):
    row_count, col_count, core_count = (lax.axis_size(a) for a in ("row", "col", "sub"))
    row_at, col_at, core = (lax.axis_index(a) for a in ("row", "col", "sub"))
    rb_dev = blocks.shape[0]
    bs_width = blocks.shape[2]
    m_loc, n_loc = vectors.shape
    total_blocks = rb_dev * row_count
    halo = BAND * bs_width
    width = n_loc // CORES
    assert core_count == CORES and width == 2 * halo and row_count == col_count * CORES
    global_rows = row_at * rb_dev + jnp.arange(rb_dev, dtype=jnp.int32)
    offset = (
        block_cols - global_rows[:, None] + total_blocks // 2
    ) % total_blocks - total_blocks // 2
    slots = offset + BAND + (jnp.arange(rb_dev, dtype=jnp.int32) % PAIR)[:, None]
    info = jnp.stack([core]).astype(jnp.int32)
    first_core = core == 0

    def other_core(x):
        return lax.ppermute(x, "sub", [(0, 1), (1, 0)])

    ring = []
    for z in range(row_count):
        ring.append((2 * z + 1, 2 * ((z + 1) % row_count)))
        ring.append((2 * ((z + 1) % row_count), 2 * z + 1))

    def exchange(parts):
        return lax.ppermute(parts[0], ("row", "sub"), ring), other_core(parts[1])

    stays = lax.dynamic_slice_in_dim(vectors, core * width, width, axis=1)
    moves = lax.dynamic_slice_in_dim(vectors, (1 - core) * width, width, axis=1)
    came = other_core(moves)
    current, halos = [], []
    for c in range(CORES):
        mine = jnp.where(core == c, stays, came)
        low, high = mine[:, :halo], mine[:, halo:]
        parts = jnp.where(first_core, low, high), jnp.where(first_core, high, low)
        current.append(parts)
        halos.append(exchange(parts))
    dense = make_dense(info, slots.reshape(-1), blocks)
    onsite = lax.dynamic_slice_in_dim(onsite, core * width, width)[None, :]

    ratio_first = half_width / (lowest - center)
    twice_inverse = 2.0 / ratio_first
    previous = [None] * CORES
    whole = [None] * CORES
    ratio_old = ratio_first
    alpha, beta = ratio_first / half_width, 0.0
    for degree_step in range(DEG):
        if degree_step:
            ratio_new = 1.0 / (twice_inverse - ratio_old)
            alpha, beta = 2.0 * ratio_new / half_width, ratio_old * ratio_new
            ratio_old = ratio_new
        last = degree_step == DEG - 1
        for c in range(CORES):
            result = apply_step(
                info, halos[c], current[c], dense, onsite, previous[c], shift=center, alpha=alpha, beta=beta, has_whole=last
            )
            previous[c], current[c] = current[c], tuple(result[:2])
            halos[c] = exchange(current[c])
            if last:
                whole[c] = result[2]

    def from_column(x, dc):
        return lax.ppermute(x, "col", [((i + dc) % col_count, i) for i in range(col_count)])

    def after(values, done):
        return lax.optimization_barrier((values, done))[0]

    peers = [[from_column(x, dc) for x in whole] for dc in range(1, col_count)]
    applied = []
    for c in range(CORES):
        result = apply_step(
            info, halos[c], current[c], dense, onsite, None, shift=0.0, alpha=1.0, beta=0.0, has_whole=True
        )
        applied.append(result[2])

    scale = gram_weight / (n_loc * row_count)
    even = row_at % 2 == 0

    def both_cores(terms):
        keep, send = terms
        return keep + other_core(send).astype(jnp.float32)

    def near_sum(rights):
        terms = both_cores(gram_terms(info, whole, rights, scale))
        a, b = terms[:m_loc], terms[m_loc:]
        send = jnp.where(even, b, a).astype(jnp.bfloat16)
        came = lax.ppermute(send, "row", [(z, z ^ 1) for z in range(row_count)])
        return jnp.where(even, a, b) + came.astype(jnp.float32)

    def far_sum(rights, peer):
        sums = []
        for c in range(CORES):
            terms = both_cores(gram_terms(info, [peer[c]], rights, scale))
            came = lax.ppermute(
                terms.astype(jnp.bfloat16), "row", [(z ^ 1, z) for z in range(c, row_count, 2)]
            )
            sums.append(terms + came.astype(jnp.float32))
        return jnp.where(even, sums[0], sums[1])

    def sum_pairs(blocks):
        count = len(blocks)
        place = row_at // 2
        if count == 1:
            return blocks[0]

        def trade(send, distance):
            pairs = [(i, i ^ distance) for i in range(row_count)]
            return lax.ppermute(send.astype(jnp.bfloat16), "row", pairs).astype(jnp.float32)

        if count == 2:
            straight = (place - col_at) % 2 == 0
            keep = jnp.where(straight, blocks[0], blocks[1])
            send = jnp.where(straight, blocks[1], blocks[0])
            return keep + trade(send, 2)
        held = jnp.stack(blocks)[(jnp.arange(count, dtype=jnp.int32) - col_at) % count]
        distance = 2
        while held.shape[0] > 1:
            held = held.reshape(held.shape[0] // 2, 2, *held.shape[1:])
            bit = (row_at // distance) % 2
            keep = lax.dynamic_index_in_dim(held, bit, 1, keepdims=False)
            send = lax.dynamic_index_in_dim(held, 1 - bit, 1, keepdims=False)
            held = keep + trade(send, distance)
            distance *= 2
        return held[0]

    near_correlation = near_sum(whole)
    near_projected = near_sum(applied)
    far_correlation = [far_sum(whole, peer) for peer in peers]
    far_projected = [far_sum(applied, peer) for peer in peers]
    return (sum_pairs([near_correlation] + far_correlation), sum_pairs([near_projected] + far_projected))


def solution(mesh):
    placed = (
        P(("kpt", "col", "sub"), "row"),
        P(("kpt", "row"), None, None, None),
        P(("kpt", "row")),
        P(("kpt", "row"), None),
    )
    return jax.shard_map(
        body,
        mesh=mesh,
        in_specs=placed,
        out_specs=(P(("kpt", "row"), ("col", "sub")), P(("kpt", "row"), ("col", "sub"))),
        check_vma=False,
    )
```
